32 devices in a mesh: gx: 8 (over y, x, core), gy: 4 (over z).
Axes of the slice: x: 2, y: 2, z: 4, core: 2. Of those that a mesh axis runs over, the one named last changes fastest.
Arguments:
- particles: float32 [8, 4, 128, 8, 128], P('gx', 'gy'), may hold values from -4 to 4, as said below
- send_list: int32 [8, 4, 4, 64], P('gx', 'gy'), may hold values from 0 to 127, as said below
- move_count: int32 [8, 4, 2, 4], P('gx', 'gy'), may hold values from 0 to 16, as said below
- tile_pairs: int32 [8, 4, 512, 2], P('gx', 'gy'), may hold values from 0 to 383, as said below
- tile_count: int32 [8, 4], P('gx', 'gy'), may hold values from 128 to 512, as said below
- drag_tiles: int32 [8, 4, 384, 4], P('gx', 'gy'), may hold values from 0 to 99, as said below
- cell_slot: int32 [8, 4, 384, 128], P('gx', 'gy'), may hold values from 0 to 511
- fluid_velocity: float32 [3, 64, 32, 128], P(None, 'gx', 'gy'), may hold values from -6 to 6
- pressure_init: float32 [64, 32, 128], P('gx', 'gy'), may hold values from -6 to 6
- source: float32 [64, 32, 128], P('gx', 'gy'), may hold values from -6 to 6
- solid_old: float32 [64, 32, 128], P('gx', 'gy'), may hold values from 0 to 0.5
- screening: float32 [64, 32, 128], P('gx', 'gy'), may hold values from 0.5 to 2
Outputs:
- pressure: float32 [64, 32, 128], P('gx', 'gy')
- drag_sum: float32 [3, 64, 32, 128], P(None, 'gx', 'gy')
- block_force: float32 [8, 4, 384, 3, 128], P('gx', 'gy')
The draws below stay inside these ranges and needn't reach their ends.
Inputs may be any that keep to these rules, and one draw needn't show every extreme that they name: `particles`: positions lie in 0 to 3, radii in 0.3 to 0.7, drag coefficients in 0.5 to 4. `send_list`: row d of a device sends toward the neighbour of higher gx (d 0), lower gx (1), higher gy (2), lower gy (3). Its first move_count[0, d] entries are blocks that move there, all different over the four rows; the others are copies, and every slot is sent. `move_count`: entry [0, d] counts blocks leaving in direction d of send_list; entry [1, d] equals entry [0, d] of the neighbour that feeds received group d (lower gx, higher gx, lower gy, higher gy). Counts toward or from outside the grid are 0; 16 is reached in every draw. `tile_pairs`: the first block of every tile slot is owned by the device after migration; the second is an own block or a slot received from a neighbour inside the grid. `tile_count`: devices at the lowest and highest gy use all 512 tiles. `drag_tiles`: the 4 columns of a block are different.
All inputs are finite; a program needn't handle non-finite values.
Results may differ from the reference program's by a relative error of at most 0.0003.
Values sent between devices are 32-bit elements; how exact they have to be, the bound alone decides.
A program may use at most 64 MiB of HBM per device.

```python
import jax
import jax.numpy as jnp
from jax import lax

CX = 8
CY = 8
NZ = 128
NB = 128
BLK = 128
K = 4
ITERS = 4
SLOTS = 64
MIGMAX = 16
POOL = 384
MAXT = 512
COLS = 100
NX = 64
NY = 32
N_GX = 8
N_GY = 4


def layout(key):
    keys = jax.random.split(jax.random.fold_in(key, 5), 6)
    grid_x = jnp.arange(N_GX)[:, None, None]
    grid_y = jnp.arange(N_GY)[None, :, None]
    heading = jnp.arange(4)[None, None, :]
    outward = (heading == 0) & (grid_x == N_GX - 1) | (heading == 1) & (grid_x == 0) | (heading == 2) & (grid_y == N_GY - 1) | (heading == 3) & (grid_y == 0)
    leave_count = jax.random.randint(keys[0], (N_GX, N_GY, 4), 0, MIGMAX + 1)
    leave_count = jnp.where(outward, 0, leave_count).at[0, 0, 0].set(MIGMAX).astype(jnp.int32)
    arrive_count = jnp.stack([jnp.roll(leave_count[:, :, 0], 1, axis=0), jnp.roll(leave_count[:, :, 1], -1, axis=0), jnp.roll(leave_count[:, :, 2], 1, axis=1), jnp.roll(leave_count[:, :, 3], -1, axis=1)], axis=-1)
    inward = jnp.stack([jnp.arange(N_GX)[:, None] > 0 + jnp.zeros((1, N_GY), jnp.int32), jnp.arange(N_GX)[:, None] < N_GX - 1 + jnp.zeros((1, N_GY), jnp.int32), jnp.arange(N_GY)[None, :] > 0 + jnp.zeros((N_GX, 1), jnp.int32), jnp.arange(N_GY)[None, :] < N_GY - 1 + jnp.zeros((N_GX, 1), jnp.int32)], axis=-1)
    scores = jax.random.randint(keys[1], (N_GX, N_GY, NB), 0, 1 << 20) * NB + jnp.arange(NB)[None, None, :]
    shuffled = jnp.argsort(scores, axis=-1).astype(jnp.int32)
    slot_iota = jnp.arange(SLOTS)[None, None, None, :]
    where_from = jnp.minimum(heading[..., None] * MIGMAX + slot_iota, NB - 1) + jnp.zeros((N_GX, N_GY, 4, SLOTS), jnp.int32)
    migrant = jnp.take_along_axis(jnp.broadcast_to(shuffled[:, :, None, :], (N_GX, N_GY, 4, NB)), where_from, axis=-1)
    copies = jax.random.randint(keys[2], (N_GX, N_GY, 4, SLOTS), 0, NB)
    send_list = jnp.where(slot_iota < leave_count[..., None], migrant, copies).astype(jnp.int32)
    leaving = (send_list[..., None] == jnp.arange(NB)[None, None, None, None, :]) & (slot_iota[..., None] < leave_count[..., None, None])
    stayed = jnp.logical_not(jnp.any(leaving, axis=(2, 3))).astype(jnp.int32)
    arrived = (slot_iota < arrive_count[..., None]).astype(jnp.int32).reshape(N_GX, N_GY, 4 * SLOTS)
    owned = jnp.concatenate([stayed, arrived], axis=-1)
    present = jnp.concatenate([jnp.ones((N_GX, N_GY, NB), jnp.int32), jnp.broadcast_to(inward[..., None], (N_GX, N_GY, 4, SLOTS)).astype(jnp.int32).reshape(N_GX, N_GY, 4 * SLOTS)], axis=-1)
    wall = (jnp.arange(N_GY)[None, :] == 0) | (jnp.arange(N_GY)[None, :] == N_GY - 1)
    wall = wall | jnp.zeros((N_GX, 1), bool)
    tile_count = jnp.where(wall, MAXT, jax.random.randint(keys[3], (N_GX, N_GY), MAXT // 4, MAXT // 2 + 1)).astype(jnp.int32)
    pool_iota = jnp.arange(POOL)[None, None, :]
    owned_order = jnp.argsort((1 - owned) * POOL + pool_iota, axis=-1)
    present_order = jnp.argsort((1 - present) * POOL + pool_iota, axis=-1)
    owned_total = jnp.sum(owned, axis=-1)
    present_total = jnp.sum(present, axis=-1)
    first_rank = jax.random.randint(keys[4], (N_GX, N_GY, MAXT), 0, owned_total[..., None])
    second_rank = jax.random.randint(keys[5], (N_GX, N_GY, MAXT), 0, present_total[..., None])
    first_block = jnp.take_along_axis(owned_order, first_rank, axis=-1)
    second_block = jnp.take_along_axis(present_order, second_rank, axis=-1)
    tile_pairs = jnp.stack([first_block, second_block], axis=-1).astype(jnp.int32)
    move_count = jnp.stack([leave_count, arrive_count], axis=2).astype(jnp.int32)
    return (send_list, move_count, tile_pairs, tile_count)


def draw_send_list(key, part):
    return layout(key)[0]


def draw_move_count(key, part):
    return layout(key)[1]


def draw_tile_pairs(key, part):
    return layout(key)[2]


def draw_tile_count(key, part):
    return layout(key)[3]


def draw_drag_tiles(key, part):
    scores = jax.random.randint(jax.random.fold_in(key, 9), (N_GX, N_GY, POOL, COLS), 0, 1 << 20) * COLS + jnp.arange(COLS)[None, None, None, :]
    return jnp.argsort(scores, axis=-1)[..., :K].astype(jnp.int32)


def draw_particles(key, part):
    keys = jax.random.split(jax.random.fold_in(key, 11), 4)
    spot_shape = (N_GX, N_GY, NB, 3, BLK)
    lone_shape = (N_GX, N_GY, NB, 1, BLK)
    spot = jax.random.uniform(keys[0], spot_shape, jnp.float32, 0.0, 3.0)
    radius = jax.random.uniform(keys[1], lone_shape, jnp.float32, 0.3, 0.7)
    speed = jnp.clip(jax.random.normal(keys[2], spot_shape, jnp.float32), -4.0, 4.0)
    coeff = jnp.exp(jax.random.uniform(keys[3], lone_shape, jnp.float32, jnp.log(0.5), jnp.log(4.0)))
    return jnp.concatenate([spot, radius, speed, coeff], axis=3).astype(jnp.float32)


def with_ends(array, key, least, top_value):
    spot = [jax.random.randint(jax.random.fold_in(key, axis), (), 0, length) for axis, length in enumerate(array.shape)]
    main_axis = array.shape.index(max(array.shape))
    beside = spot[:main_axis] + [(spot[main_axis] + 1) % array.shape[main_axis]] + spot[main_axis + 1:]
    return array.at[tuple(spot)].set(least).at[tuple(beside)].set(top_value)


def block_scale(rng, extent, cuts, least, high):
    level = 1.0
    for dim, blocks in cuts:
        steps = jax.random.uniform(jax.random.fold_in(jax.random.fold_in(rng, 6), dim), (blocks,), jnp.float32, least / len(cuts), high / len(cuts))
        level = level * jnp.repeat(jnp.exp(steps), extent[dim] // blocks).reshape((-1,) + (1,) * (len(extent) - 1 - dim))
    return level


def gaussian(rng, extent, deviation, bound, cuts=(), kind=jnp.bfloat16):
    entries = deviation * jax.random.normal(rng, extent, jnp.float32)
    if cuts:
        entries = entries * block_scale(rng, extent, cuts, -0.22, 0.18)
    return jnp.clip(entries, -bound, bound).astype(kind)


def setup_inputs(seed: int = 0) -> dict:
    key_of = jax.random.split(jax.random.key(seed), 13)
    particles = draw_particles(jax.random.fold_in(key_of[12], 71), 0)
    send_list = draw_send_list(jax.random.fold_in(key_of[12], 71), 0)
    move_count = draw_move_count(jax.random.fold_in(key_of[12], 71), 0)
    tile_pairs = draw_tile_pairs(jax.random.fold_in(key_of[12], 71), 0)
    tile_count = draw_tile_count(jax.random.fold_in(key_of[12], 71), 0)
    drag_tiles = draw_drag_tiles(jax.random.fold_in(key_of[12], 71), 0)
    cell_slot = with_ends(jax.random.randint(key_of[6], (N_GX, N_GY, POOL, BLK), 0, K * NZ), jax.random.fold_in(key_of[6], 1), 0, (K * NZ) - 1).astype(jnp.int32)
    fluid_velocity = gaussian(key_of[7], (3, NX, NY, NZ), 1.0, 6.0, ((1, 8), (2, 4)), jnp.float32)
    pressure_init = gaussian(key_of[8], (NX, NY, NZ), 1.0, 6.0, ((0, 8), (1, 4)), jnp.float32)
    source = gaussian(key_of[9], (NX, NY, NZ), 1.0, 6.0, ((0, 8), (1, 4)), jnp.float32)
    solid_old = jnp.clip(0.5 * jax.random.uniform(key_of[10], (NX, NY, NZ), jnp.float32) ** block_scale(key_of[10], (NX, NY, NZ), ((0, 8), (1, 4)), -0.2, 0.2), 0.0, 0.5)
    screening = jnp.clip(0.5 + 1.5 * jax.random.uniform(key_of[11], (NX, NY, NZ), jnp.float32) ** block_scale(key_of[11], (NX, NY, NZ), ((0, 8), (1, 4)), -0.2, 0.2), 0.5, 2.0)
    return dict(particles=particles, send_list=send_list, move_count=move_count, tile_pairs=tile_pairs, tile_count=tile_count, drag_tiles=drag_tiles, cell_slot=cell_slot, fluid_velocity=fluid_velocity, pressure_init=pressure_init, source=source, solid_old=solid_old, screening=screening)


topmost_value = lax.Precision.HIGHEST
stiffness = 0.5
density_ratio = 2.0
tile_group = 32
block_groups = 6


def gather_pool(particles, send_list, grid_x, grid_y):
    own_blocks = particles[grid_x, grid_y]
    pieces = [own_blocks]
    for step_x, step_y, heading in ((-1, 0, 0), (1, 0, 1), (0, -1, 2), (0, 1, 3)):
        source_x = grid_x + step_x
        source_y = grid_y + step_y
        inside = (source_x >= 0) & (source_x < N_GX) & (source_y >= 0) & (source_y < N_GY)
        clip_x = jnp.clip(source_x, 0, N_GX - 1)
        clip_y = jnp.clip(source_y, 0, N_GY - 1)
        picked = particles[clip_x, clip_y][send_list[clip_x, clip_y, heading]]
        pieces.append(jnp.where(inside, picked, jnp.zeros_like(picked)))
    return jnp.concatenate(pieces, axis=0)


def ownership(send_rows, leave_count, arrive_count, block_count):
    slot_count = send_rows.shape[1]
    slot_iota = jnp.arange(slot_count, dtype=jnp.int32)
    leaving = (send_rows[:, :, None] == jnp.arange(block_count, dtype=jnp.int32)[None, None, :]) & (slot_iota[None, :, None] < leave_count[:, None, None])
    stayed = jnp.logical_not(jnp.any(leaving, axis=(0, 1)))
    arrived = slot_iota[None, :] < arrive_count[:, None]
    return jnp.concatenate([stayed, arrived.reshape(-1)]).astype(jnp.float32)


def contact_forces(block_pool, tile_rows, tile_total):
    slot_total = tile_rows.shape[0]
    grouped = tile_rows.reshape(slot_total // tile_group, tile_group, 2)
    marks = (jnp.arange(slot_total, dtype=jnp.int32) < tile_total).astype(jnp.float32).reshape(-1, tile_group)

    def tile_step(force_total, step_item):
        pair_group, mark_group = step_item
        first_side = block_pool[pair_group[:, 0], 0:4, :]
        second_side = block_pool[pair_group[:, 1], 0:4, :]
        distance = (first_side[:, 0, :, None] - second_side[:, 0, None, :]) ** 2
        distance = distance + (first_side[:, 1, :, None] - second_side[:, 1, None, :]) ** 2
        distance = distance + (first_side[:, 2, :, None] - second_side[:, 2, None, :]) ** 2
        reach = first_side[:, 3, :, None] + second_side[:, 3, None, :]
        weight = jnp.maximum(1.0 - distance / (reach * reach), 0.0) * mark_group[:, None, None]
        pulled = jnp.einsum('tab,tcb->tca', weight, second_side[:, 0:3, :], precision=topmost_value)
        pushed = first_side[:, 0:3, :] * jnp.sum(weight, axis=2)[:, None, :]
        return force_total.at[pair_group[:, 0]].add(stiffness * (pushed - pulled)), None

    start_force = jnp.zeros((block_pool.shape[0], 3, block_pool.shape[2]), jnp.float32)
    force_total, unused = lax.scan(tile_step, start_force, (grouped, marks))
    return force_total


def couple(block_pool, owned_mask, tile_ids, slot_ids, columns):
    depth_count = columns.shape[2]
    column_count = columns.shape[0]
    tile_width = tile_ids.shape[1]
    per_group = block_pool.shape[0] // block_groups

    def group_advance(deposit, step_item):
        block_state, owned_rows, group_tiles, group_slots = step_item
        depth_ids = group_slots % depth_count
        slot_tile = group_slots // depth_count
        depth_pick = (depth_ids[:, :, None] == jnp.arange(depth_count, dtype=jnp.int32)[None, None, :]).astype(jnp.float32)
        slot_selection = (slot_tile[:, :, None] == jnp.arange(tile_width, dtype=jnp.int32)[None, None, :]).astype(jnp.float32)
        local_flow = columns[group_tiles]
        depth_position = jnp.einsum('gkcz,gpz->gkcp', local_flow, depth_pick, precision=topmost_value)
        fluid_sampled_locally = jnp.einsum('hxdq,hqx->hdq', depth_position, slot_selection, precision=topmost_value)
        drag_force = block_state[:, 7:8, :] * (fluid_sampled_locally - block_state[:, 4:7, :]) * owned_rows[:, None, None]
        volume = block_state[:, 3:4, :] ** 3 * owned_rows[:, None, None]
        loading_contributions = jnp.concatenate([drag_force, volume], axis=1)
        slot_breakdown = jnp.einsum('bfm,bmd->bdfm', loading_contributions, slot_selection, precision=topmost_value)
        spread = jnp.einsum('gkcp,gpz->gkcz', slot_breakdown, depth_pick, precision=topmost_value)
        column_pick = (group_tiles[:, :, None] == jnp.arange(column_count, dtype=jnp.int32)[None, None, :]).astype(jnp.float32)
        deposit = deposit + jnp.einsum('gkn,gkcz->ncz', column_pick, spread, precision=topmost_value)
        return deposit, drag_force

    step_items = (block_pool.reshape(block_groups, per_group, block_pool.shape[1], block_pool.shape[2]),
                  owned_mask.reshape(block_groups, per_group),
                  tile_ids.reshape(block_groups, per_group, tile_width),
                  slot_ids.reshape(block_groups, per_group, slot_ids.shape[1]))
    start_deposit = jnp.zeros((column_count, 4, depth_count), jnp.float32)
    deposit, drag_force = lax.scan(group_advance, start_deposit, step_items)
    return drag_force.reshape(block_pool.shape[0], 3, block_pool.shape[2]), deposit


def reference(particles, send_list, move_count, tile_pairs, tile_count, drag_tiles, cell_slot, fluid_velocity, pressure_init, source, solid_old, screening):
    flow_padded = jnp.pad(fluid_velocity, ((0, 0), (1, 1), (1, 1), (0, 0)))
    column_count = (CX + 2) * (CY + 2)
    zero_index = jnp.zeros((), jnp.int32)

    def per_device(device_flat):
        grid_x = (device_flat // N_GY).astype(jnp.int32)
        grid_y = (device_flat % N_GY).astype(jnp.int32)
        block_pool = gather_pool(particles, send_list, grid_x, grid_y)
        owned_mask = ownership(send_list[grid_x, grid_y], move_count[grid_x, grid_y, 0], move_count[grid_x, grid_y, 1], NB)
        contact = contact_forces(block_pool, tile_pairs[grid_x, grid_y], tile_count[grid_x, grid_y])
        window = lax.dynamic_slice(flow_padded, (zero_index, grid_x * CX, grid_y * CY, zero_index), (3, CX + 2, CY + 2, NZ))
        columns = window.reshape(3, column_count, NZ).transpose(1, 0, 2)
        drag_force, deposit = couple(block_pool, owned_mask, drag_tiles[grid_x, grid_y], cell_slot[grid_x, grid_y], columns)
        return contact + drag_force, deposit.transpose(1, 0, 2).reshape(4, CX + 2, CY + 2, NZ)

    forces, deposits = lax.map(per_device, jnp.arange(N_GX * N_GY, dtype=jnp.int32))

    def place(device_flat, field):
        grid_x = (device_flat // N_GY).astype(jnp.int32)
        grid_y = (device_flat % N_GY).astype(jnp.int32)
        corner = (zero_index, grid_x * CX, grid_y * CY, zero_index)
        current = lax.dynamic_slice(field, corner, (4, CX + 2, CY + 2, NZ))
        return lax.dynamic_update_slice(field, current + deposits[device_flat], corner)

    field = lax.fori_loop(0, N_GX * N_GY, place, jnp.zeros((4, NX + 2, NY + 2, NZ), jnp.float32))
    loads = field[:, 1:-1, 1:-1]
    drag_sum = loads[0:3]
    relax_gain = 1.0 / (6.0 + screening)
    offset = relax_gain * (source + density_ratio * (loads[3] - solid_old))
    pressure = pressure_init
    for sweep_turn in range(ITERS):
        padded = jnp.pad(pressure, 1)
        neighbours = padded[2:, 1:-1, 1:-1] + padded[:-2, 1:-1, 1:-1]
        neighbours = neighbours + padded[1:-1, 2:, 1:-1] + padded[1:-1, :-2, 1:-1]
        neighbours = neighbours + padded[1:-1, 1:-1, 2:] + padded[1:-1, 1:-1, :-2]
        pressure = relax_gain * neighbours + offset
    return pressure, drag_sum, forces.reshape(N_GX, N_GY, POOL, 3, BLK)
```

```python
import functools

import jax
import jax.numpy as jnp
from jax import lax
from jax.experimental import pallas as pl
from jax.experimental.pallas import tpu as pltpu
from jax.sharding import PartitionSpec as P

ITERS = 4
MOVERS = 16
WIDE = ITERS
UNROLL = 8
MESH = pl.DeviceIdType.MESH
AROUND = [(dx, dy) for dx in (-1, 0, 1) for dy in (-1, 0, 1) if (dx, dy) != (0, 0)]
GROUPS = [(1, 0), (-1, 0), (0, 1), (0, -1)]
f32, bf16 = jnp.float32, jnp.bfloat16
VM = pltpu.VMEM
LIMIT = 48 * 1024 * 1024


def span(step, count, width):
    if step == 0:
        return 0, count
    return (count - width, width) if step > 0 else (0, width)


def place(step, count, width):
    if step == 0:
        return width, count
    return (width + count, width) if step > 0 else (0, width)


def neighbour(step, n_x, n_y):
    a, b = lax.axis_index("gx") + step[0], lax.axis_index("gy") + step[1]
    return (a >= 0) & (a < n_x) & (b >= 0) & (b < n_y), (a, b)


def enter(n_x, n_y):
    barrier = pltpu.get_barrier_semaphore()
    for step in AROUND:
        there, device = neighbour(step, n_x, n_y)

        @pl.when(there)
        def _():
            pl.semaphore_signal(barrier, inc=1, device_id=device, device_id_type=MESH)

    peers = 0
    for step in AROUND:
        there, device = neighbour(step, n_x, n_y)
        peers = peers + there.astype(jnp.int32)
    pl.semaphore_wait(barrier, peers)


def pick_kernel(send_ref, own_ref, out_ref):
    total = out_ref.shape[0]

    def step(s, carry):
        for u in range(8):
            out_ref[s * 8 + u] = own_ref[send_ref[s * 8 + u]]
        return carry

    lax.fori_loop(0, total // 8, step, 0)


def exchange_kernel(n_x, n_y, blocks, flow, press, screen, source, solid,
                    got, columns, p_ext, g_ext, s_ext, *scratch):
    n = len(AROUND)
    wide_out, wide_in = scratch[0:n], scratch[n:2 * n]
    slim_out, slim_in = scratch[2 * n:3 * n], scratch[3 * n:4 * n]
    sends, recvs = scratch[4 * n:]
    cx, cy = press.shape[0], press.shape[1]
    enter(n_x, n_y)

    def block_copy(d):
        there, device = neighbour(GROUPS[d], n_x, n_y)
        return there, pltpu.make_async_remote_copy(
            src_ref=blocks.at[d], dst_ref=got.at[d], send_sem=sends.at[2 * n + d],
            recv_sem=recvs.at[2 * n + d], device_id=device, device_id_type=MESH)

    for d in (2, 3, 0, 1):
        there, copy = block_copy(d)

        @pl.when(there)
        def _():
            copy.start()

    gain = 1.0 / (6.0 + screen[...])
    rest = source[...] - 2.0 * solid[...]
    g_ext[...] = jnp.zeros(g_ext.shape, f32)
    s_ext[...] = jnp.zeros(s_ext.shape, f32)
    p_ext[...] = jnp.zeros(p_ext.shape, f32)
    g_ext[WIDE:WIDE + cx, WIDE:WIDE + cy, :] = gain
    s_ext[WIDE:WIDE + cx, WIDE:WIDE + cy, :] = rest
    p_ext[WIDE:WIDE + cx, WIDE:WIDE + cy, :] = press[...]

    def halo_copies(e):
        there, device = neighbour(AROUND[e], n_x, n_y)
        back = AROUND.index((-AROUND[e][0], -AROUND[e][1]))
        kw = dict(device_id=device, device_id_type=MESH)
        return there, [
            pltpu.make_async_remote_copy(src_ref=wide_out[e], dst_ref=wide_in[back],
                                         send_sem=sends.at[e], recv_sem=recvs.at[back], **kw),
            pltpu.make_async_remote_copy(src_ref=slim_out[e], dst_ref=slim_in[back],
                                         send_sem=sends.at[n + e], recv_sem=recvs.at[n + back],
                                         **kw)]

    for e, (dx, dy) in enumerate(AROUND):
        x0, xn = span(dx, cx, WIDE)
        y0, yn = span(dy, cy, WIDE)
        wide_out[e][0] = press[x0:x0 + xn, y0:y0 + yn, :]
        wide_out[e][1] = gain[x0:x0 + xn, y0:y0 + yn, :]
        wide_out[e][2] = rest[x0:x0 + xn, y0:y0 + yn, :]
        x0, xn = span(dx, cx, 1)
        y0, yn = span(dy, cy, 1)
        for c in range(3):
            if dx and dy:
                slim_out[e][c:c + 1, :] = flow[c, x0, y0:y0 + 1, :]
            elif dx:
                slim_out[e][c] = flow[c, x0]
            else:
                for x in range(cx):
                    slim_out[e][c, x:x + 1, :] = flow[c, x, y0:y0 + 1, :]
        there, copies = halo_copies(e)

        @pl.when(there)
        def _():
            for copy in copies:
                copy.start()

    columns[...] = jnp.zeros(columns.shape, f32)
    for c in range(3):
        for x in range(cx):
            first = ((x + 1) * (cy + 2) + 1) * 8 + c
            columns[pl.ds(first, cy, stride=8), :] = flow[c, x]

    for d in range(4):
        there, copy = block_copy(d)
        back = (-GROUPS[d][0], -GROUPS[d][1])
        fed, unused = neighbour(back, n_x, n_y)

        @pl.when(jnp.logical_not(fed))
        def _():
            got[d] = jnp.zeros(got.shape[1:], f32)

    for e, (dx, dy) in enumerate(AROUND):
        there, copies = halo_copies(e)
        back = AROUND.index((-dx, -dy))

        @pl.when(there)
        def _():
            here, from_it = halo_copies(back)
            for copy in from_it:
                copy.wait_recv()
            x0, xn = place(dx, cx, WIDE)
            y0, yn = place(dy, cy, WIDE)
            p_ext[x0:x0 + xn, y0:y0 + yn, :] = wide_in[e][0]
            g_ext[x0:x0 + xn, y0:y0 + yn, :] = wide_in[e][1]
            s_ext[x0:x0 + xn, y0:y0 + yn, :] = wide_in[e][2]
            x0, xn = place(dx, cx, 1)
            y0, yn = place(dy, cy, 1)
            for c in range(3):
                if dx and dy:
                    columns[pl.ds((x0 * (cy + 2) + y0) * 8 + c, 1), :] = slim_in[e][c:c + 1, :]
                elif dx:
                    first = (x0 * (cy + 2) + 1) * 8 + c
                    columns[pl.ds(first, cy, stride=8), :] = slim_in[e][c]
                else:
                    first = ((cy + 2) + y0) * 8 + c
                    columns[pl.ds(first, cx, stride=8 * (cy + 2)), :] = slim_in[e][c]
            for copy in copies:
                copy.wait_send()

    for d in range(4):
        there, copy = block_copy(d)
        fed, unused = neighbour((-GROUPS[d][0], -GROUPS[d][1]), n_x, n_y)

        @pl.when(fed)
        def _():
            copy.wait_recv()

        @pl.when(there)
        def _():
            copy.wait_send()


def split3(value):
    high = value.astype(bf16).astype(f32)
    rest = value - high
    mid = rest.astype(bf16).astype(f32)
    return high, mid, (rest - mid).astype(bf16).astype(f32)


def forces_kernel(pairs, count, tiles, send, moves, own, got, cells, columns,
                  deposit, force, owned, tab_a, tab_b, tab_y, total, drag, dep):
    n_own, slots = own.shape[0], got.shape[1]
    pool = n_own + 4 * slots
    cx, cy = deposit.shape[1], deposit.shape[2]
    depth = cells.shape[1]
    row = lax.broadcasted_iota(jnp.int32, (8, depth), 0)
    low = row < 4
    deep = lax.broadcasted_iota(jnp.int32, (depth, depth), 0)

    def mark(k, carry):
        owned[k] = 1.0
        return carry

    lax.fori_loop(0, n_own, mark, 0)
    for d in range(4):
        def unmark(s, carry):
            owned[send[d * slots + s]] = 0.0
            return carry

        lax.fori_loop(0, moves[d], unmark, 0)
    dep[...] = jnp.zeros(dep.shape, f32)
    total[...] = jnp.zeros(total.shape, f32)

    def tables(m, block):
        both = jnp.where(low, block, pltpu.roll(block, 4, 0))
        c1, c2, c3 = split3(both)
        square = jnp.where(row < 3, -both * both, jnp.where(row == 3, both * both, 0.0))
        n1, n2, n3 = split3(jnp.sum(square, axis=0, keepdims=True))
        ones = jnp.ones((8, depth), f32)
        zeros = jnp.zeros((8, depth), f32)
        a3 = jnp.where(row == 0, n1, jnp.where(row == 1, n2, jnp.where(row == 2, n3, jnp.where(row < 6, ones, zeros))))
        b3 = jnp.where(row == 3, n1, jnp.where(row == 4, n2, jnp.where(row == 5, n3, jnp.where(row < 3, ones, zeros))))
        a = jnp.concatenate([c1, c2, jnp.where(low, c1, c3), a3], axis=0)
        twice = 2.0 * jnp.where(low, c1, c2)
        b = jnp.concatenate([twice, twice, 2.0 * jnp.where(low, c3, c1), b3], axis=0)
        third = jnp.where(row == 3, ones, zeros)
        r1, r2, r3 = c1[3:4], c2[3:4], c3[3:4]
        reach = jnp.where(row == 3, r1, jnp.where(row == 4, r2, jnp.where(row == 5, r3, zeros)))
        r = jnp.concatenate([third, third, jnp.where(row == 7, ones, zeros), reach], axis=0)
        y1 = jnp.where(row < 3, c1, jnp.where(row == 3, ones, jnp.where(row < 7, c2, zeros)))
        y2 = jnp.where(row < 3, c1, jnp.where(row == 3, ones, zeros))
        y = jnp.concatenate([jnp.concatenate([y1, y2], axis=1),
                             jnp.zeros((8, 2 * depth), f32)], axis=0)
        tab_a[m] = a.astype(bf16)
        tab_b[m] = jnp.concatenate([b, r], axis=1).astype(bf16)
        tab_y[m] = y.astype(bf16)

    def drag_block(m, block, cell, mine):
        slot = cell // depth
        z = cell - slot * depth
        index = jnp.broadcast_to(z, (8, depth))
        slot8 = jnp.broadcast_to(slot, (8, depth))
        fluid = jnp.zeros((8, depth), f32)
        where = [pl.multiple_of(tiles[m * 4 + k] * 8, 8) for k in range(4)]
        for k in range(4):
            at = jnp.take_along_axis(columns[pl.ds(where[k], 8), :], index, axis=1)
            fluid = jnp.where(slot8 == k, at, fluid)
        pull = block[7:8, :] * (fluid - pltpu.roll(block, 4, 0))
        load = jnp.where(row < 3, pull, jnp.where(low, block * block * block, 0.0)) * mine
        drag[m] = load
        high = load.astype(bf16).astype(f32)
        parts = jnp.where(low, high, pltpu.roll(load - high, 4, 0))
        left = jnp.concatenate([jnp.where(slot8 == k, parts, 0.0) for k in range(4)], axis=0)
        hot = jnp.where(deep == z, 1.0, 0.0).astype(bf16)
        out = lax.dot_general(left.astype(bf16), hot, (((1,), (1,)), ((), ())),
                              preferred_element_type=f32)
        return where, out

    def deposit_all(results):
        for where, out in results:
            for k in range(4):
                dep[pl.ds(where[k], 8), :] += out[8 * k:8 * k + 8]

    def own_step(s, carry):
        cell8 = cells[pl.ds(pl.multiple_of(s * 8, 8), 8), :]
        results = []
        for u in range(8):
            m = s * 8 + u
            block = own[m]
            tables(m, block)
            results.append(drag_block(m, block, cell8[u:u + 1], owned[m]))
        deposit_all(results)
        return carry

    lax.fori_loop(0, n_own // 8, own_step, 0)
    for d in range(4):
        def got_step(s, carry):
            base = n_own + d * slots
            cell8 = cells[pl.ds(pl.multiple_of(base + s * 8, 8), 8), :]
            results = []
            for u in range(8):
                k = s * 8 + u
                mine = jnp.where(k < moves[4 + d], 1.0, 0.0).astype(f32)
                results.append(drag_block(base + k, got[d, k], cell8[u:u + 1], mine))
            deposit_all(results)
            return carry

        lax.fori_loop(0, MOVERS // 8, got_step, 0)

        def table_step(s, carry):
            for u in range(8):
                tables(n_own + d * slots + s * 8 + u, got[d, s * 8 + u])
            return carry

        lax.fori_loop(0, slots // 8, table_step, 0)

    for c in range(4):
        for x in range(cx):
            high = dep[pl.ds(x * cy * 8 + c, cy, stride=8), :]
            rest = dep[pl.ds(x * cy * 8 + 4 + c, cy, stride=8), :]
            deposit[c, x] = high + rest

    def tile_step(s, carry):
        results = []
        for u in range(UNROLL):
            t = s * UNROLL + u
            i, j = pairs[2 * t], pairs[2 * t + 1]
            mr = lax.dot_general(tab_a[j], tab_b[i], (((0,), (0,)), ((), ())),
                                 preferred_element_type=f32)
            over, reach = mr[:, :depth], mr[:, depth:]
            inverse = pl.reciprocal(reach, approx=True)
            inverse = inverse * (2.0 - reach * inverse)
            weight = jnp.maximum(over, 0.0) * (inverse * inverse)
            w1 = weight.astype(bf16)
            w2 = (weight - w1.astype(f32)).astype(bf16)
            out = lax.dot_general(tab_y[j], jnp.concatenate([w1, w2], axis=0),
                                  (((1,), (0,)), ((), ())), preferred_element_type=f32)
            keep = jnp.where(t < count[0], 1.0, 0.0).astype(f32)
            results.append((i, out[0:8] * keep))
        for i, out in results:
            total[i] += out
        return carry

    lax.fori_loop(0, (count[0] + UNROLL - 1) // UNROLL, tile_step, 0)

    def finish(m, block):
        sums = total[m]
        sums = sums + pltpu.roll(sums, 4, 0)
        contact = 0.5 * (block * sums[3:4] - sums)
        force[m] = (contact + drag[m])[0:3]

    def own_finish(s, carry):
        for u in range(8):
            finish(s * 8 + u, own[s * 8 + u])
        return carry

    lax.fori_loop(0, n_own // 8, own_finish, 0)
    for d in range(4):
        def got_finish(s, carry):
            for u in range(8):
                finish(n_own + d * slots + s * 8 + u, got[d, s * 8 + u])
            return carry

        lax.fori_loop(0, MOVERS // 8, got_finish, 0)
        force[pl.ds(n_own + d * slots + MOVERS, slots - MOVERS)] = jnp.zeros(
            (slots - MOVERS, 3, depth), f32)


def pressure_kernel(n_x, n_y, deposit, p_ext, g_ext, s_ext, press, drag_sum, load, *scratch):
    n = len(AROUND)
    wide_out, wide_in = scratch[0:n], scratch[n:2 * n]
    slim_out, slim_in = scratch[2 * n:3 * n], scratch[3 * n:4 * n]
    sends, recvs = scratch[4 * n:]
    cx, cy = press.shape[0], press.shape[1]

    def copies_of(e):
        there, device = neighbour(AROUND[e], n_x, n_y)
        back = AROUND.index((-AROUND[e][0], -AROUND[e][1]))
        kw = dict(device_id=device, device_id_type=MESH)
        return there, [
            pltpu.make_async_remote_copy(src_ref=wide_out[e], dst_ref=wide_in[back],
                                         send_sem=sends.at[e], recv_sem=recvs.at[back], **kw),
            pltpu.make_async_remote_copy(src_ref=slim_out[e], dst_ref=slim_in[back],
                                         send_sem=sends.at[n + e], recv_sem=recvs.at[n + back],
                                         **kw)]

    for e, (dx, dy) in enumerate(AROUND):
        x0, xn = span(dx, cx + 2, WIDE)
        y0, yn = span(dy, cy + 2, WIDE)
        wide_out[e][...] = deposit[3, x0:x0 + xn, y0:y0 + yn, :]
        x0 = cx + 1 if dx > 0 else 0
        y0 = cy + 1 if dy > 0 else 0
        for c in range(3):
            if dx and dy:
                slim_out[e][c:c + 1, :] = deposit[c, x0, y0:y0 + 1, :]
            elif dx:
                slim_out[e][c] = deposit[c, x0, 1:1 + cy, :]
            else:
                for x in range(cx):
                    slim_out[e][c, x:x + 1, :] = deposit[c, x + 1, y0:y0 + 1, :]
    enter(n_x, n_y)
    for e in range(n):
        there, copies = copies_of(e)

        @pl.when(there)
        def _():
            for copy in copies:
                copy.start()

    load[...] = jnp.zeros(load.shape, f32)
    load[WIDE - 1:WIDE + cx + 1, WIDE - 1:WIDE + cy + 1, :] = deposit[3]
    drag_sum[...] = deposit[0:3, 1:1 + cx, 1:1 + cy, :]

    def put(step, count):
        if step == 0:
            return WIDE - 1, count + 2
        return (WIDE + count - 1, WIDE) if step > 0 else (1, WIDE)

    for e, (dx, dy) in enumerate(AROUND):
        there, copies = copies_of(e)
        back = AROUND.index((-dx, -dy))

        @pl.when(there)
        def _():
            here, from_it = copies_of(back)
            for copy in from_it:
                copy.wait_recv()
            x0, xn = put(dx, cx)
            y0, yn = put(dy, cy)
            load[x0:x0 + xn, y0:y0 + yn, :] += wide_in[e][...]
            x0 = cx - 1 if dx > 0 else 0
            y0 = cy - 1 if dy > 0 else 0
            for c in range(3):
                if dx and dy:
                    drag_sum[c, x0, y0:y0 + 1, :] += slim_in[e][c:c + 1, :]
                elif dx:
                    drag_sum[c, x0] += slim_in[e][c]
                else:
                    for x in range(cx):
                        drag_sum[c, x, y0:y0 + 1, :] += slim_in[e][c, x:x + 1, :]
            for copy in copies:
                copy.wait_send()

    gain = g_ext[...]
    offset = gain * (s_ext[...] + 2.0 * load[...])
    value = p_ext[...]
    wx, wy, depth = value.shape
    lane = lax.broadcasted_iota(jnp.int32, (wx * wy, depth), 1)
    first, last = lane == 0, lane == depth - 1
    edge_x = jnp.zeros((1, wy, depth), f32)
    for sweep in range(ITERS):
        flat = value.reshape(wx * wy, depth)
        near = (jnp.where(first, 0.0, pltpu.roll(flat, 1, 1))
                + jnp.where(last, 0.0, pltpu.roll(flat, depth - 1, 1)))
        near = near + pltpu.roll(flat, 1, 0) + pltpu.roll(flat, wx * wy - 1, 0)
        near = near.reshape(wx, wy, depth)
        near = near + jnp.concatenate([edge_x, value[:-1]], axis=0)
        near = near + jnp.concatenate([value[1:], edge_x], axis=0)
        value = gain * near + offset
    press[...] = value[WIDE:WIDE + cx, WIDE:WIDE + cy, :]


def shapes(cx, cy, depth, thick):
    wide = [VM(thick + (cx if dx == 0 else WIDE, cy if dy == 0 else WIDE, depth), f32)
            for dx, dy in AROUND]
    return wide + wide


def slim_shapes(cx, cy, depth):
    slim = [VM((8, depth), f32) if dx and dy else VM((3, cy if dx else cx, depth), f32)
            for dx, dy in AROUND]
    return slim + slim


def body(n_x, n_y, particles, send_list, move_count, tile_pairs, tile_count, drag_tiles,
         cell_slot, fluid_velocity, pressure_init, source, solid_old, screening):
    own = particles[0, 0]
    n_own, comps, width = own.shape
    slots = send_list.shape[3]
    pool = n_own + 4 * slots
    cx, cy, depth = pressure_init.shape
    n = len(AROUND)
    send = send_list.reshape(-1)
    sds = jax.ShapeDtypeStruct
    vmem = pl.BlockSpec(memory_space=VM)
    smem = pl.BlockSpec(memory_space=pltpu.SMEM)

    blocks = pl.pallas_call(
        pick_kernel, out_shape=sds((4 * slots, comps, width), f32),
        in_specs=[smem, vmem], out_specs=vmem,
    )(send, own).reshape(4, slots, comps, width)

    ext = (cx + 2 * WIDE, cy + 2 * WIDE, depth)
    column_rows = (cx + 2) * (cy + 2) * 8
    got, columns, p_ext, g_ext, s_ext = pl.pallas_call(
        functools.partial(exchange_kernel, n_x, n_y),
        out_shape=[sds((4, slots, comps, width), f32), sds((column_rows, depth), f32),
                   sds(ext, f32), sds(ext, f32), sds(ext, f32)],
        in_specs=[vmem] * 6, out_specs=[vmem] * 5,
        scratch_shapes=shapes(cx, cy, depth, (3,)) + slim_shapes(cx, cy, depth)
        + [pltpu.SemaphoreType.DMA((2 * n + 4,)), pltpu.SemaphoreType.DMA((2 * n + 4,))],
        compiler_params=pltpu.CompilerParams(collective_id=0, has_side_effects=True,
                                             vmem_limit_bytes=LIMIT),
    )(blocks, fluid_velocity, pressure_init, screening, source, solid_old)

    deposit, force = pl.pallas_call(
        forces_kernel,
        out_shape=[sds((4, cx + 2, cy + 2, depth), f32), sds((pool, 3, width), f32)],
        in_specs=[smem] * 5 + [vmem] * 4, out_specs=[vmem] * 2,
        scratch_shapes=[pltpu.SMEM((n_own,), f32), VM((pool, 32, width), bf16),
                        VM((pool, 32, 2 * width), bf16), VM((pool, 16, 2 * width), bf16),
                        VM((pool, 8, width), f32), VM((pool, 8, width), f32),
                        VM((column_rows, depth), f32)],
        compiler_params=pltpu.CompilerParams(vmem_limit_bytes=LIMIT),
    )(tile_pairs.reshape(-1), tile_count.reshape(-1), drag_tiles.reshape(-1), send,
      move_count.reshape(-1), own, got, cell_slot[0, 0], columns)

    press, drag_sum = pl.pallas_call(
        functools.partial(pressure_kernel, n_x, n_y),
        out_shape=[sds((cx, cy, depth), f32), sds((3, cx, cy, depth), f32)],
        in_specs=[vmem] * 4, out_specs=[vmem] * 2,
        scratch_shapes=[VM(ext, f32)] + shapes(cx + 2, cy + 2, depth, ())
        + slim_shapes(cx, cy, depth)
        + [pltpu.SemaphoreType.DMA((2 * n,)), pltpu.SemaphoreType.DMA((2 * n,))],
        compiler_params=pltpu.CompilerParams(collective_id=1, has_side_effects=True,
                                             vmem_limit_bytes=LIMIT),
    )(deposit, p_ext, g_ext, s_ext)
    return press, drag_sum, force[None, None]


def solution(mesh):
    tail = P("gx", "gy", None)
    in_specs = (
        P("gx", "gy", None, None, None),
        P("gx", "gy", None, None),
        P("gx", "gy", None, None),
        P("gx", "gy", None, None),
        P("gx", "gy"),
        P("gx", "gy", None, None),
        P("gx", "gy", None, None),
        P(None, "gx", "gy", None),
        tail, tail, tail, tail,
    )
    out_specs = (tail, P(None, "gx", "gy", None), P("gx", "gy", None, None, None))
    return jax.shard_map(functools.partial(body, mesh.shape["gx"], mesh.shape["gy"]), mesh=mesh,
                         in_specs=in_specs, out_specs=out_specs, check_vma=False)
```

```python
import functools

import jax
import jax.numpy as jnp
from jax import lax
from jax.experimental import pallas as pl
from jax.experimental.pallas import tpu as pltpu
from jax.sharding import PartitionSpec as P

ITERS = 4
MOVERS = 16
WIDE = ITERS
UNROLL = 8
MESH = pl.DeviceIdType.MESH
AROUND = [(dx, dy) for dx in (-1, 0, 1) for dy in (-1, 0, 1) if (dx, dy) != (0, 0)]
GROUPS = [(1, 0), (-1, 0), (0, 1), (0, -1)]
f32, bf16 = jnp.float32, jnp.bfloat16
VM = pltpu.VMEM
LIMIT = 48 * 1024 * 1024


def span(step, count, width):
    if step == 0:
        return 0, count
    return (count - width, width) if step > 0 else (0, width)


def place(step, count, width):
    if step == 0:
        return width, count
    return (width + count, width) if step > 0 else (0, width)


def neighbour(step, n_x, n_y):
    a, b = lax.axis_index("gx") + step[0], lax.axis_index("gy") + step[1]
    return (a >= 0) & (a < n_x) & (b >= 0) & (b < n_y), (a, b)


def enter(n_x, n_y):
    barrier = pltpu.get_barrier_semaphore()
    for step in AROUND:
        there, device = neighbour(step, n_x, n_y)

        @pl.when(there)
        def _():
            pl.semaphore_signal(barrier, inc=1, device_id=device, device_id_type=MESH)

    peers = 0
    for step in AROUND:
        there, device = neighbour(step, n_x, n_y)
        peers = peers + there.astype(jnp.int32)
    pl.semaphore_wait(barrier, peers)


def pick_kernel(send_ref, own_ref, out_ref):
    total = out_ref.shape[0]

    def step(s, carry):
        for u in range(8):
            out_ref[s * 8 + u] = own_ref[send_ref[s * 8 + u]]
        return carry

    lax.fori_loop(0, total // 8, step, 0)


def exchange_kernel(n_x, n_y, blocks, flow, press, screen, source, solid,
                    got, columns, p_ext, g_ext, s_ext, *scratch):
    n = len(AROUND)
    wide_out, wide_in = scratch[0:n], scratch[n:2 * n]
    slim_out, slim_in = scratch[2 * n:3 * n], scratch[3 * n:4 * n]
    sends, recvs = scratch[4 * n:]
    cx, cy = press.shape[0], press.shape[1]
    enter(n_x, n_y)

    def block_copy(d):
        there, device = neighbour(GROUPS[d], n_x, n_y)
        return there, pltpu.make_async_remote_copy(
            src_ref=blocks.at[d], dst_ref=got.at[d], send_sem=sends.at[2 * n + d],
            recv_sem=recvs.at[2 * n + d], device_id=device, device_id_type=MESH)

    for d in (2, 3, 0, 1):
        there, copy = block_copy(d)

        @pl.when(there)
        def _():
            copy.start()

    gain = 1.0 / (6.0 + screen[...])
    rest = source[...] - 2.0 * solid[...]
    g_ext[...] = jnp.zeros(g_ext.shape, f32)
    s_ext[...] = jnp.zeros(s_ext.shape, f32)
    p_ext[...] = jnp.zeros(p_ext.shape, f32)
    g_ext[WIDE:WIDE + cx, WIDE:WIDE + cy, :] = gain
    s_ext[WIDE:WIDE + cx, WIDE:WIDE + cy, :] = rest
    p_ext[WIDE:WIDE + cx, WIDE:WIDE + cy, :] = press[...]

    def halo_copies(e):
        there, device = neighbour(AROUND[e], n_x, n_y)
        back = AROUND.index((-AROUND[e][0], -AROUND[e][1]))
        kw = dict(device_id=device, device_id_type=MESH)
        return there, [
            pltpu.make_async_remote_copy(src_ref=wide_out[e], dst_ref=wide_in[back],
                                         send_sem=sends.at[e], recv_sem=recvs.at[back], **kw),
            pltpu.make_async_remote_copy(src_ref=slim_out[e], dst_ref=slim_in[back],
                                         send_sem=sends.at[n + e], recv_sem=recvs.at[n + back],
                                         **kw)]

    for e, (dx, dy) in enumerate(AROUND):
        x0, xn = span(dx, cx, WIDE)
        y0, yn = span(dy, cy, WIDE)
        wide_out[e][0] = press[x0:x0 + xn, y0:y0 + yn, :]
        wide_out[e][1] = gain[x0:x0 + xn, y0:y0 + yn, :]
        wide_out[e][2] = rest[x0:x0 + xn, y0:y0 + yn, :]
        x0, xn = span(dx, cx, 1)
        y0, yn = span(dy, cy, 1)
        for c in range(3):
            if dx and dy:
                slim_out[e][c:c + 1, :] = flow[c, x0, y0:y0 + 1, :]
            elif dx:
                slim_out[e][c] = flow[c, x0]
            else:
                for x in range(cx):
                    slim_out[e][c, x:x + 1, :] = flow[c, x, y0:y0 + 1, :]
        there, copies = halo_copies(e)

        @pl.when(there)
        def _():
            for copy in copies:
                copy.start()

    columns[...] = jnp.zeros(columns.shape, f32)
    for c in range(3):
        for x in range(cx):
            first = ((x + 1) * (cy + 2) + 1) * 8 + c
            columns[pl.ds(first, cy, stride=8), :] = flow[c, x]

    for d in range(4):
        there, copy = block_copy(d)
        back = (-GROUPS[d][0], -GROUPS[d][1])
        fed, unused = neighbour(back, n_x, n_y)

        @pl.when(jnp.logical_not(fed))
        def _():
            got[d] = jnp.zeros(got.shape[1:], f32)

    for e, (dx, dy) in enumerate(AROUND):
        there, copies = halo_copies(e)
        back = AROUND.index((-dx, -dy))

        @pl.when(there)
        def _():
            here, from_it = halo_copies(back)
            for copy in from_it:
                copy.wait_recv()
            x0, xn = place(dx, cx, WIDE)
            y0, yn = place(dy, cy, WIDE)
            p_ext[x0:x0 + xn, y0:y0 + yn, :] = wide_in[e][0]
            g_ext[x0:x0 + xn, y0:y0 + yn, :] = wide_in[e][1]
            s_ext[x0:x0 + xn, y0:y0 + yn, :] = wide_in[e][2]
            x0, xn = place(dx, cx, 1)
            y0, yn = place(dy, cy, 1)
            for c in range(3):
                if dx and dy:
                    columns[pl.ds((x0 * (cy + 2) + y0) * 8 + c, 1), :] = slim_in[e][c:c + 1, :]
                elif dx:
                    first = (x0 * (cy + 2) + 1) * 8 + c
                    columns[pl.ds(first, cy, stride=8), :] = slim_in[e][c]
                else:
                    first = ((cy + 2) + y0) * 8 + c
                    columns[pl.ds(first, cx, stride=8 * (cy + 2)), :] = slim_in[e][c]
            for copy in copies:
                copy.wait_send()

    for d in range(4):
        there, copy = block_copy(d)
        fed, unused = neighbour((-GROUPS[d][0], -GROUPS[d][1]), n_x, n_y)

        @pl.when(fed)
        def _():
            copy.wait_recv()

        @pl.when(there)
        def _():
            copy.wait_send()


def forces_kernel(pairs, count, tiles, send, moves, own, got, cells, columns,
                  deposit, force, owned, whole, column, tab_y, total, drag, dep):
    n_own, slots = own.shape[0], got.shape[1]
    pool = n_own + 4 * slots
    cx, cy = deposit.shape[1], deposit.shape[2]
    depth = cells.shape[1]
    row = lax.broadcasted_iota(jnp.int32, (8, depth), 0)
    low = row < 4
    deep = lax.broadcasted_iota(jnp.int32, (depth, depth), 0)

    def mark(k, carry):
        owned[k] = 1.0
        return carry

    lax.fori_loop(0, n_own, mark, 0)
    for d in range(4):
        def unmark(s, carry):
            owned[send[d * slots + s]] = 0.0
            return carry

        lax.fori_loop(0, moves[d], unmark, 0)
    dep[...] = jnp.zeros(dep.shape, f32)
    total[...] = jnp.zeros(total.shape, f32)

    def tables(m, block):
        whole[m] = block
        column[m] = block.T
        ones = jnp.where(row < 3, block, jnp.where(row == 3, 1.0, 0.0))
        high = ones.astype(bf16).astype(f32)
        rest = pltpu.roll(ones - high, 4, 0)
        high = jnp.where(row < 4, high, 0.0)
        y = jnp.concatenate([jnp.where(low, high, rest), high], axis=1)
        tab_y[m] = jnp.concatenate([y, jnp.zeros((8, 2 * depth), f32)], axis=0).astype(bf16)

    def drag_block(m, block, cell, mine):
        slot = cell // depth
        z = cell - slot * depth
        index = jnp.broadcast_to(z, (8, depth))
        slot8 = jnp.broadcast_to(slot, (8, depth))
        fluid = jnp.zeros((8, depth), f32)
        where = [pl.multiple_of(tiles[m * 4 + k] * 8, 8) for k in range(4)]
        for k in range(4):
            at = jnp.take_along_axis(columns[pl.ds(where[k], 8), :], index, axis=1)
            fluid = jnp.where(slot8 == k, at, fluid)
        pull = block[7:8, :] * (fluid - pltpu.roll(block, 4, 0))
        load = jnp.where(row < 3, pull, jnp.where(low, block * block * block, 0.0)) * mine
        drag[m] = load
        high = load.astype(bf16).astype(f32)
        parts = jnp.where(low, high, pltpu.roll(load - high, 4, 0))
        left = jnp.concatenate([jnp.where(slot8 == k, parts, 0.0) for k in range(4)], axis=0)
        hot = jnp.where(deep == z, 1.0, 0.0).astype(bf16)
        out = lax.dot_general(left.astype(bf16), hot, (((1,), (1,)), ((), ())),
                              preferred_element_type=f32)
        return where, out

    def deposit_all(results):
        for where, out in results:
            for k in range(4):
                dep[pl.ds(where[k], 8), :] += out[8 * k:8 * k + 8]

    def own_step(s, carry):
        cell8 = cells[pl.ds(pl.multiple_of(s * 8, 8), 8), :]
        results = []
        for u in range(8):
            m = s * 8 + u
            block = own[m]
            tables(m, block)
            results.append(drag_block(m, block, cell8[u:u + 1], owned[m]))
        deposit_all(results)
        return carry

    lax.fori_loop(0, n_own // 8, own_step, 0)
    for d in range(4):
        def got_step(s, carry):
            base = n_own + d * slots
            cell8 = cells[pl.ds(pl.multiple_of(base + s * 8, 8), 8), :]
            results = []
            for u in range(8):
                k = s * 8 + u
                mine = jnp.where(k < moves[4 + d], 1.0, 0.0).astype(f32)
                results.append(drag_block(base + k, got[d, k], cell8[u:u + 1], mine))
            deposit_all(results)
            return carry

        lax.fori_loop(0, MOVERS // 8, got_step, 0)

        def table_step(s, carry):
            for u in range(8):
                tables(n_own + d * slots + s * 8 + u, got[d, s * 8 + u])
            return carry

        lax.fori_loop(0, slots // 8, table_step, 0)

    for c in range(4):
        for x in range(cx):
            high = dep[pl.ds(x * cy * 8 + c, cy, stride=8), :]
            rest = dep[pl.ds(x * cy * 8 + 4 + c, cy, stride=8), :]
            deposit[c, x] = high + rest

    def tile_step(s, carry):
        results = []
        for u in range(UNROLL):
            t = s * UNROLL + u
            i, j = pairs[2 * t], pairs[2 * t + 1]
            first, second = whole[i], column[j]
            gap = [second[:, c:c + 1] - first[c:c + 1, :] for c in range(3)]
            apart = gap[0] * gap[0] + gap[1] * gap[1] + gap[2] * gap[2]
            reach = second[:, 3:4] + first[3:4, :]
            reach = reach * reach
            inverse = pl.reciprocal(reach, approx=True)
            weight = jnp.maximum(1.0 - apart * inverse, 0.0)
            w1 = weight.astype(bf16)
            w2 = (weight - w1.astype(f32)).astype(bf16)
            out = lax.dot_general(tab_y[j], jnp.concatenate([w1, w2], axis=0),
                                  (((1,), (0,)), ((), ())), preferred_element_type=f32)
            keep = jnp.where(t < count[0], 1.0, 0.0).astype(f32)
            results.append((i, out[0:8] * keep))
        for i, out in results:
            total[i] += out
        return carry

    lax.fori_loop(0, (count[0] + UNROLL - 1) // UNROLL, tile_step, 0)

    def finish(m, block):
        sums = total[m]
        sums = sums + pltpu.roll(sums, 4, 0)
        contact = 0.5 * (block * sums[3:4] - sums)
        force[m] = (contact + drag[m])[0:3]

    def own_finish(s, carry):
        for u in range(8):
            finish(s * 8 + u, own[s * 8 + u])
        return carry

    lax.fori_loop(0, n_own // 8, own_finish, 0)
    for d in range(4):
        def got_finish(s, carry):
            for u in range(8):
                finish(n_own + d * slots + s * 8 + u, got[d, s * 8 + u])
            return carry

        lax.fori_loop(0, MOVERS // 8, got_finish, 0)
        force[pl.ds(n_own + d * slots + MOVERS, slots - MOVERS)] = jnp.zeros(
            (slots - MOVERS, 3, depth), f32)


def pressure_kernel(n_x, n_y, deposit, p_ext, g_ext, s_ext, press, drag_sum, load, *scratch):
    n = len(AROUND)
    wide_out, wide_in = scratch[0:n], scratch[n:2 * n]
    slim_out, slim_in = scratch[2 * n:3 * n], scratch[3 * n:4 * n]
    sends, recvs = scratch[4 * n:]
    cx, cy = press.shape[0], press.shape[1]

    def copies_of(e):
        there, device = neighbour(AROUND[e], n_x, n_y)
        back = AROUND.index((-AROUND[e][0], -AROUND[e][1]))
        kw = dict(device_id=device, device_id_type=MESH)
        return there, [
            pltpu.make_async_remote_copy(src_ref=wide_out[e], dst_ref=wide_in[back],
                                         send_sem=sends.at[e], recv_sem=recvs.at[back], **kw),
            pltpu.make_async_remote_copy(src_ref=slim_out[e], dst_ref=slim_in[back],
                                         send_sem=sends.at[n + e], recv_sem=recvs.at[n + back],
                                         **kw)]

    for e, (dx, dy) in enumerate(AROUND):
        x0, xn = span(dx, cx + 2, WIDE)
        y0, yn = span(dy, cy + 2, WIDE)
        wide_out[e][...] = deposit[3, x0:x0 + xn, y0:y0 + yn, :]
        x0 = cx + 1 if dx > 0 else 0
        y0 = cy + 1 if dy > 0 else 0
        for c in range(3):
            if dx and dy:
                slim_out[e][c:c + 1, :] = deposit[c, x0, y0:y0 + 1, :]
            elif dx:
                slim_out[e][c] = deposit[c, x0, 1:1 + cy, :]
            else:
                for x in range(cx):
                    slim_out[e][c, x:x + 1, :] = deposit[c, x + 1, y0:y0 + 1, :]
    enter(n_x, n_y)
    for e in range(n):
        there, copies = copies_of(e)

        @pl.when(there)
        def _():
            for copy in copies:
                copy.start()

    load[...] = jnp.zeros(load.shape, f32)
    load[WIDE - 1:WIDE + cx + 1, WIDE - 1:WIDE + cy + 1, :] = deposit[3]
    drag_sum[...] = deposit[0:3, 1:1 + cx, 1:1 + cy, :]

    def put(step, count):
        if step == 0:
            return WIDE - 1, count + 2
        return (WIDE + count - 1, WIDE) if step > 0 else (1, WIDE)

    for e, (dx, dy) in enumerate(AROUND):
        there, copies = copies_of(e)
        back = AROUND.index((-dx, -dy))

        @pl.when(there)
        def _():
            here, from_it = copies_of(back)
            for copy in from_it:
                copy.wait_recv()
            x0, xn = put(dx, cx)
            y0, yn = put(dy, cy)
            load[x0:x0 + xn, y0:y0 + yn, :] += wide_in[e][...]
            x0 = cx - 1 if dx > 0 else 0
            y0 = cy - 1 if dy > 0 else 0
            for c in range(3):
                if dx and dy:
                    drag_sum[c, x0, y0:y0 + 1, :] += slim_in[e][c:c + 1, :]
                elif dx:
                    drag_sum[c, x0] += slim_in[e][c]
                else:
                    for x in range(cx):
                        drag_sum[c, x, y0:y0 + 1, :] += slim_in[e][c, x:x + 1, :]
            for copy in copies:
                copy.wait_send()

    gain = g_ext[...]
    offset = gain * (s_ext[...] + 2.0 * load[...])
    value = p_ext[...]
    wx, wy, depth = value.shape
    lane = lax.broadcasted_iota(jnp.int32, (wx * wy, depth), 1)
    first, last = lane == 0, lane == depth - 1
    edge_x = jnp.zeros((1, wy, depth), f32)
    for sweep in range(ITERS):
        flat = value.reshape(wx * wy, depth)
        near = (jnp.where(first, 0.0, pltpu.roll(flat, 1, 1))
                + jnp.where(last, 0.0, pltpu.roll(flat, depth - 1, 1)))
        near = near + pltpu.roll(flat, 1, 0) + pltpu.roll(flat, wx * wy - 1, 0)
        near = near.reshape(wx, wy, depth)
        near = near + jnp.concatenate([edge_x, value[:-1]], axis=0)
        near = near + jnp.concatenate([value[1:], edge_x], axis=0)
        value = gain * near + offset
    press[...] = value[WIDE:WIDE + cx, WIDE:WIDE + cy, :]


def shapes(cx, cy, depth, thick):
    wide = [VM(thick + (cx if dx == 0 else WIDE, cy if dy == 0 else WIDE, depth), f32)
            for dx, dy in AROUND]
    return wide + wide


def slim_shapes(cx, cy, depth):
    slim = [VM((8, depth), f32) if dx and dy else VM((3, cy if dx else cx, depth), f32)
            for dx, dy in AROUND]
    return slim + slim


def body(n_x, n_y, particles, send_list, move_count, tile_pairs, tile_count, drag_tiles,
         cell_slot, fluid_velocity, pressure_init, source, solid_old, screening):
    own = particles[0, 0]
    n_own, comps, width = own.shape
    slots = send_list.shape[3]
    pool = n_own + 4 * slots
    cx, cy, depth = pressure_init.shape
    n = len(AROUND)
    send = send_list.reshape(-1)
    sds = jax.ShapeDtypeStruct
    vmem = pl.BlockSpec(memory_space=VM)
    smem = pl.BlockSpec(memory_space=pltpu.SMEM)

    blocks = pl.pallas_call(
        pick_kernel, out_shape=sds((4 * slots, comps, width), f32),
        in_specs=[smem, vmem], out_specs=vmem,
    )(send, own).reshape(4, slots, comps, width)

    ext = (cx + 2 * WIDE, cy + 2 * WIDE, depth)
    column_rows = (cx + 2) * (cy + 2) * 8
    got, columns, p_ext, g_ext, s_ext = pl.pallas_call(
        functools.partial(exchange_kernel, n_x, n_y),
        out_shape=[sds((4, slots, comps, width), f32), sds((column_rows, depth), f32),
                   sds(ext, f32), sds(ext, f32), sds(ext, f32)],
        in_specs=[vmem] * 6, out_specs=[vmem] * 5,
        scratch_shapes=shapes(cx, cy, depth, (3,)) + slim_shapes(cx, cy, depth)
        + [pltpu.SemaphoreType.DMA((2 * n + 4,)), pltpu.SemaphoreType.DMA((2 * n + 4,))],
        compiler_params=pltpu.CompilerParams(collective_id=0, has_side_effects=True,
                                             vmem_limit_bytes=LIMIT),
    )(blocks, fluid_velocity, pressure_init, screening, source, solid_old)

    deposit, force = pl.pallas_call(
        forces_kernel,
        out_shape=[sds((4, cx + 2, cy + 2, depth), f32), sds((pool, 3, width), f32)],
        in_specs=[smem] * 5 + [vmem] * 4, out_specs=[vmem] * 2,
        scratch_shapes=[pltpu.SMEM((n_own,), f32), VM((pool, comps, width), f32),
                        VM((pool, width, comps), f32), VM((pool, 16, 2 * width), bf16),
                        VM((pool, 8, width), f32), VM((pool, 8, width), f32),
                        VM((column_rows, depth), f32)],
        compiler_params=pltpu.CompilerParams(vmem_limit_bytes=LIMIT),
    )(tile_pairs.reshape(-1), tile_count.reshape(-1), drag_tiles.reshape(-1), send,
      move_count.reshape(-1), own, got, cell_slot[0, 0], columns)

    press, drag_sum = pl.pallas_call(
        functools.partial(pressure_kernel, n_x, n_y),
        out_shape=[sds((cx, cy, depth), f32), sds((3, cx, cy, depth), f32)],
        in_specs=[vmem] * 4, out_specs=[vmem] * 2,
        scratch_shapes=[VM(ext, f32)] + shapes(cx + 2, cy + 2, depth, ())
        + slim_shapes(cx, cy, depth)
        + [pltpu.SemaphoreType.DMA((2 * n,)), pltpu.SemaphoreType.DMA((2 * n,))],
        compiler_params=pltpu.CompilerParams(collective_id=1, has_side_effects=True,
                                             vmem_limit_bytes=LIMIT),
    )(deposit, p_ext, g_ext, s_ext)
    return press, drag_sum, force[None, None]


def solution(mesh):
    tail = P("gx", "gy", None)
    in_specs = (
        P("gx", "gy", None, None, None),
        P("gx", "gy", None, None),
        P("gx", "gy", None, None),
        P("gx", "gy", None, None),
        P("gx", "gy"),
        P("gx", "gy", None, None),
        P("gx", "gy", None, None),
        P(None, "gx", "gy", None),
        tail, tail, tail, tail,
    )
    out_specs = (tail, P(None, "gx", "gy", None), P("gx", "gy", None, None, None))
    return jax.shard_map(functools.partial(body, mesh.shape["gx"], mesh.shape["gy"]), mesh=mesh,
                         in_specs=in_specs, out_specs=out_specs, check_vma=False)
```

```python
import functools

import jax
import jax.numpy as jnp
from jax import lax
from jax.experimental import pallas as pl
from jax.experimental.pallas import tpu as pltpu
from jax.sharding import PartitionSpec as P

ITERS = 4
MOVERS = 16
WIDE = ITERS
UNROLL = 16
CHUNK = 16
MESH = pl.DeviceIdType.MESH
AROUND = [(dx, dy) for dx in (-1, 0, 1) for dy in (-1, 0, 1) if (dx, dy) != (0, 0)]
GROUPS = [(1, 0), (-1, 0), (0, 1), (0, -1)]
f32, bf16 = jnp.float32, jnp.bfloat16
VM = pltpu.VMEM
LIMIT = 48 * 1024 * 1024


def span(step, count, width):
    if step == 0:
        return 0, count
    return (count - width, width) if step > 0 else (0, width)


def place(step, count, width):
    if step == 0:
        return width, count
    return (width + count, width) if step > 0 else (0, width)


def neighbour(step, n_x, n_y):
    a, b = lax.axis_index("gx") + step[0], lax.axis_index("gy") + step[1]
    return (a >= 0) & (a < n_x) & (b >= 0) & (b < n_y), (a, b)


def enter(n_x, n_y):
    barrier = pltpu.get_barrier_semaphore()
    for step in AROUND:
        there, device = neighbour(step, n_x, n_y)

        @pl.when(there)
        def _():
            pl.semaphore_signal(barrier, inc=1, device_id=device, device_id_type=MESH)

    peers = 0
    for step in AROUND:
        there, device = neighbour(step, n_x, n_y)
        peers = peers + there.astype(jnp.int32)
    pl.semaphore_wait(barrier, peers)


def pick_kernel(send_ref, own_ref, out_ref):
    total = out_ref.shape[0]

    def step(s, carry):
        for u in range(8):
            out_ref[s * 8 + u] = own_ref[send_ref[s * 8 + u]]
        return carry

    lax.fori_loop(0, total // 8, step, 0)


def exchange_kernel(n_x, n_y, blocks, flow, press, screen, source, solid,
                    got, columns, p_ext, g_ext, s_ext, *scratch):
    n = len(AROUND)
    wide_out, wide_in = scratch[0:n], scratch[n:2 * n]
    slim_out, slim_in = scratch[2 * n:3 * n], scratch[3 * n:4 * n]
    sends, recvs = scratch[4 * n:]
    cx, cy = press.shape[0], press.shape[1]
    enter(n_x, n_y)

    def block_copy(d):
        there, device = neighbour(GROUPS[d], n_x, n_y)
        return there, pltpu.make_async_remote_copy(
            src_ref=blocks.at[d], dst_ref=got.at[d], send_sem=sends.at[2 * n + d],
            recv_sem=recvs.at[2 * n + d], device_id=device, device_id_type=MESH)

    for d in (2, 3, 0, 1):
        there, copy = block_copy(d)

        @pl.when(there)
        def _():
            copy.start()

    gain = 1.0 / (6.0 + screen[...])
    rest = source[...] - 2.0 * solid[...]
    g_ext[...] = jnp.zeros(g_ext.shape, f32)
    s_ext[...] = jnp.zeros(s_ext.shape, f32)
    p_ext[...] = jnp.zeros(p_ext.shape, f32)
    g_ext[WIDE:WIDE + cx, WIDE:WIDE + cy, :] = gain
    s_ext[WIDE:WIDE + cx, WIDE:WIDE + cy, :] = rest
    p_ext[WIDE:WIDE + cx, WIDE:WIDE + cy, :] = press[...]

    def halo_copies(e):
        there, device = neighbour(AROUND[e], n_x, n_y)
        back = AROUND.index((-AROUND[e][0], -AROUND[e][1]))
        kw = dict(device_id=device, device_id_type=MESH)
        return there, [
            pltpu.make_async_remote_copy(src_ref=wide_out[e], dst_ref=wide_in[back],
                                         send_sem=sends.at[e], recv_sem=recvs.at[back], **kw),
            pltpu.make_async_remote_copy(src_ref=slim_out[e], dst_ref=slim_in[back],
                                         send_sem=sends.at[n + e], recv_sem=recvs.at[n + back],
                                         **kw)]

    for e, (dx, dy) in enumerate(AROUND):
        x0, xn = span(dx, cx, WIDE)
        y0, yn = span(dy, cy, WIDE)
        wide_out[e][0] = press[x0:x0 + xn, y0:y0 + yn, :]
        wide_out[e][1] = gain[x0:x0 + xn, y0:y0 + yn, :]
        wide_out[e][2] = rest[x0:x0 + xn, y0:y0 + yn, :]
        x0, xn = span(dx, cx, 1)
        y0, yn = span(dy, cy, 1)
        for c in range(3):
            if dx and dy:
                slim_out[e][c:c + 1, :] = flow[c, x0, y0:y0 + 1, :]
            elif dx:
                slim_out[e][c] = flow[c, x0]
            else:
                for x in range(cx):
                    slim_out[e][c, x:x + 1, :] = flow[c, x, y0:y0 + 1, :]
        there, copies = halo_copies(e)

        @pl.when(there)
        def _():
            for copy in copies:
                copy.start()

    columns[...] = jnp.zeros(columns.shape, f32)
    for c in range(3):
        for x in range(cx):
            first = ((x + 1) * (cy + 2) + 1) * 8 + c
            columns[pl.ds(first, cy, stride=8), :] = flow[c, x]

    for d in range(4):
        there, copy = block_copy(d)
        back = (-GROUPS[d][0], -GROUPS[d][1])
        fed, unused = neighbour(back, n_x, n_y)

        @pl.when(jnp.logical_not(fed))
        def _():
            got[d] = jnp.zeros(got.shape[1:], f32)

    for e, (dx, dy) in enumerate(AROUND):
        there, copies = halo_copies(e)
        back = AROUND.index((-dx, -dy))

        @pl.when(there)
        def _():
            here, from_it = halo_copies(back)
            for copy in from_it:
                copy.wait_recv()
            x0, xn = place(dx, cx, WIDE)
            y0, yn = place(dy, cy, WIDE)
            p_ext[x0:x0 + xn, y0:y0 + yn, :] = wide_in[e][0]
            g_ext[x0:x0 + xn, y0:y0 + yn, :] = wide_in[e][1]
            s_ext[x0:x0 + xn, y0:y0 + yn, :] = wide_in[e][2]
            x0, xn = place(dx, cx, 1)
            y0, yn = place(dy, cy, 1)
            for c in range(3):
                if dx and dy:
                    columns[pl.ds((x0 * (cy + 2) + y0) * 8 + c, 1), :] = slim_in[e][c:c + 1, :]
                elif dx:
                    first = (x0 * (cy + 2) + 1) * 8 + c
                    columns[pl.ds(first, cy, stride=8), :] = slim_in[e][c]
                else:
                    first = ((cy + 2) + y0) * 8 + c
                    columns[pl.ds(first, cx, stride=8 * (cy + 2)), :] = slim_in[e][c]
            for copy in copies:
                copy.wait_send()

    for d in range(4):
        there, copy = block_copy(d)
        fed, unused = neighbour((-GROUPS[d][0], -GROUPS[d][1]), n_x, n_y)

        @pl.when(fed)
        def _():
            copy.wait_recv()

        @pl.when(there)
        def _():
            copy.wait_send()


def forces_kernel(pairs, count, tiles, send, moves, own, got, cells, columns,
                  deposit, force, owned, whole, column, tab_y, total, drag, dep):
    n_own, slots = own.shape[0], got.shape[1]
    pool = n_own + 4 * slots
    cx, cy = deposit.shape[1], deposit.shape[2]
    depth = cells.shape[1]
    row = lax.broadcasted_iota(jnp.int32, (8, depth), 0)
    low = row < 4
    deep = lax.broadcasted_iota(jnp.int32, (depth, depth), 0)

    def mark(k, carry):
        owned[k] = 1.0
        return carry

    lax.fori_loop(0, n_own, mark, 0)
    for d in range(4):
        def unmark(s, carry):
            owned[send[d * slots + s]] = 0.0
            return carry

        lax.fori_loop(0, moves[d], unmark, 0)
    dep[...] = jnp.zeros(dep.shape, f32)
    total[...] = jnp.zeros(total.shape, f32)

    def tables(m, block):
        whole[m] = block
        column[m] = block.T
        ones = jnp.where(row < 3, block, jnp.where(row == 3, 1.0, 0.0))
        high = ones.astype(bf16).astype(f32)
        rest = pltpu.roll(ones - high, 4, 0)
        high = jnp.where(row < 4, high, 0.0)
        y = jnp.concatenate([jnp.where(low, high, rest), high], axis=1)
        tab_y[m] = jnp.concatenate([y, jnp.zeros((8, 2 * depth), f32)], axis=0).astype(bf16)

    def drag_block(m, block, cell, mine):
        slot = cell // depth
        z = cell - slot * depth
        index = jnp.broadcast_to(z, (8, depth))
        slot8 = jnp.broadcast_to(slot, (8, depth))
        fluid = jnp.zeros((8, depth), f32)
        where = [pl.multiple_of(tiles[m * 4 + k] * 8, 8) for k in range(4)]
        for k in range(4):
            at = jnp.take_along_axis(columns[pl.ds(where[k], 8), :], index, axis=1)
            fluid = jnp.where(slot8 == k, at, fluid)
        pull = block[7:8, :] * (fluid - pltpu.roll(block, 4, 0))
        load = jnp.where(row < 3, pull, jnp.where(low, block * block * block, 0.0)) * mine
        drag[m] = load
        high = load.astype(bf16).astype(f32)
        parts = jnp.where(low, high, pltpu.roll(load - high, 4, 0))
        left = jnp.concatenate([jnp.where(slot8 == k, parts, 0.0) for k in range(4)], axis=0)
        hot = jnp.where(deep == z, 1.0, 0.0).astype(bf16)
        out = lax.dot_general(left.astype(bf16), hot, (((1,), (1,)), ((), ())),
                              preferred_element_type=f32)
        return where, out

    def deposit_all(results):
        for where, out in results:
            for k in range(4):
                dep[pl.ds(where[k], 8), :] += out[8 * k:8 * k + 8]

    def own_step(s, carry):
        cell8 = cells[pl.ds(pl.multiple_of(s * 8, 8), 8), :]
        results = []
        for u in range(8):
            m = s * 8 + u
            block = own[m]
            tables(m, block)
            results.append(drag_block(m, block, cell8[u:u + 1], owned[m]))
        deposit_all(results)
        return carry

    lax.fori_loop(0, n_own // 8, own_step, 0)
    for d in range(4):
        def got_step(s, carry):
            base = n_own + d * slots
            cell8 = cells[pl.ds(pl.multiple_of(base + s * 8, 8), 8), :]
            results = []
            for u in range(8):
                k = s * 8 + u
                mine = jnp.where(k < moves[4 + d], 1.0, 0.0).astype(f32)
                results.append(drag_block(base + k, got[d, k], cell8[u:u + 1], mine))
            deposit_all(results)
            return carry

        lax.fori_loop(0, MOVERS // 8, got_step, 0)

        def table_step(s, carry):
            for u in range(8):
                tables(n_own + d * slots + s * 8 + u, got[d, s * 8 + u])
            return carry

        lax.fori_loop(0, slots // 8, table_step, 0)

    for c in range(4):
        for x in range(cx):
            high = dep[pl.ds(x * cy * 8 + c, cy, stride=8), :]
            rest = dep[pl.ds(x * cy * 8 + 4 + c, cy, stride=8), :]
            deposit[c, x] = high + rest

    def tile_step(s, carry):
        results = []
        for u in range(UNROLL):
            t = s * UNROLL + u
            i, j = pairs[2 * t], pairs[2 * t + 1]
            first, second = whole[i], column[j]
            highs, rests = [], []
            for h in range(0, depth, CHUNK):
                part = second[h:h + CHUNK]
                gap = [part[:, c:c + 1] - first[c:c + 1, :] for c in range(3)]
                apart = gap[0] * gap[0] + gap[1] * gap[1] + gap[2] * gap[2]
                reach = part[:, 3:4] + first[3:4, :]
                inverse = pl.reciprocal(reach * reach, approx=True)
                weight = jnp.maximum(1.0 - apart * inverse, 0.0)
                high = weight.astype(bf16)
                highs.append(high)
                rests.append((weight - high.astype(f32)).astype(bf16))
            out = lax.dot_general(tab_y[j], jnp.concatenate(highs + rests, axis=0),
                                  (((1,), (0,)), ((), ())), preferred_element_type=f32)
            keep = jnp.where(t < count[0], 1.0, 0.0).astype(f32)
            results.append((i, out[0:8] * keep))
        for i, out in results:
            total[i] += out
        return carry

    lax.fori_loop(0, (count[0] + UNROLL - 1) // UNROLL, tile_step, 0)

    def finish(m, block):
        sums = total[m]
        sums = sums + pltpu.roll(sums, 4, 0)
        contact = 0.5 * (block * sums[3:4] - sums)
        force[m] = (contact + drag[m])[0:3]

    def own_finish(s, carry):
        for u in range(8):
            finish(s * 8 + u, own[s * 8 + u])
        return carry

    lax.fori_loop(0, n_own // 8, own_finish, 0)
    for d in range(4):
        def got_finish(s, carry):
            for u in range(8):
                finish(n_own + d * slots + s * 8 + u, got[d, s * 8 + u])
            return carry

        lax.fori_loop(0, MOVERS // 8, got_finish, 0)
        force[pl.ds(n_own + d * slots + MOVERS, slots - MOVERS)] = jnp.zeros(
            (slots - MOVERS, 3, depth), f32)


def pressure_kernel(n_x, n_y, deposit, p_ext, g_ext, s_ext, press, drag_sum, load, *scratch):
    n = len(AROUND)
    wide_out, wide_in = scratch[0:n], scratch[n:2 * n]
    slim_out, slim_in = scratch[2 * n:3 * n], scratch[3 * n:4 * n]
    sends, recvs = scratch[4 * n:]
    cx, cy = press.shape[0], press.shape[1]

    def copies_of(e):
        there, device = neighbour(AROUND[e], n_x, n_y)
        back = AROUND.index((-AROUND[e][0], -AROUND[e][1]))
        kw = dict(device_id=device, device_id_type=MESH)
        return there, [
            pltpu.make_async_remote_copy(src_ref=wide_out[e], dst_ref=wide_in[back],
                                         send_sem=sends.at[e], recv_sem=recvs.at[back], **kw),
            pltpu.make_async_remote_copy(src_ref=slim_out[e], dst_ref=slim_in[back],
                                         send_sem=sends.at[n + e], recv_sem=recvs.at[n + back],
                                         **kw)]

    for e, (dx, dy) in enumerate(AROUND):
        x0, xn = span(dx, cx + 2, WIDE)
        y0, yn = span(dy, cy + 2, WIDE)
        wide_out[e][...] = deposit[3, x0:x0 + xn, y0:y0 + yn, :]
        x0 = cx + 1 if dx > 0 else 0
        y0 = cy + 1 if dy > 0 else 0
        for c in range(3):
            if dx and dy:
                slim_out[e][c:c + 1, :] = deposit[c, x0, y0:y0 + 1, :]
            elif dx:
                slim_out[e][c] = deposit[c, x0, 1:1 + cy, :]
            else:
                for x in range(cx):
                    slim_out[e][c, x:x + 1, :] = deposit[c, x + 1, y0:y0 + 1, :]
    enter(n_x, n_y)
    for e in range(n):
        there, copies = copies_of(e)

        @pl.when(there)
        def _():
            for copy in copies:
                copy.start()

    load[...] = jnp.zeros(load.shape, f32)
    load[WIDE - 1:WIDE + cx + 1, WIDE - 1:WIDE + cy + 1, :] = deposit[3]
    drag_sum[...] = deposit[0:3, 1:1 + cx, 1:1 + cy, :]

    def put(step, count):
        if step == 0:
            return WIDE - 1, count + 2
        return (WIDE + count - 1, WIDE) if step > 0 else (1, WIDE)

    for e, (dx, dy) in enumerate(AROUND):
        there, copies = copies_of(e)
        back = AROUND.index((-dx, -dy))

        @pl.when(there)
        def _():
            here, from_it = copies_of(back)
            for copy in from_it:
                copy.wait_recv()
            x0, xn = put(dx, cx)
            y0, yn = put(dy, cy)
            load[x0:x0 + xn, y0:y0 + yn, :] += wide_in[e][...]
            x0 = cx - 1 if dx > 0 else 0
            y0 = cy - 1 if dy > 0 else 0
            for c in range(3):
                if dx and dy:
                    drag_sum[c, x0, y0:y0 + 1, :] += slim_in[e][c:c + 1, :]
                elif dx:
                    drag_sum[c, x0] += slim_in[e][c]
                else:
                    for x in range(cx):
                        drag_sum[c, x, y0:y0 + 1, :] += slim_in[e][c, x:x + 1, :]
            for copy in copies:
                copy.wait_send()

    gain = g_ext[...]
    offset = gain * (s_ext[...] + 2.0 * load[...])
    value = p_ext[...]
    wx, wy, depth = value.shape
    lane = lax.broadcasted_iota(jnp.int32, (wx * wy, depth), 1)
    first, last = lane == 0, lane == depth - 1
    edge_x = jnp.zeros((1, wy, depth), f32)
    for sweep in range(ITERS):
        flat = value.reshape(wx * wy, depth)
        near = (jnp.where(first, 0.0, pltpu.roll(flat, 1, 1))
                + jnp.where(last, 0.0, pltpu.roll(flat, depth - 1, 1)))
        near = near + pltpu.roll(flat, 1, 0) + pltpu.roll(flat, wx * wy - 1, 0)
        near = near.reshape(wx, wy, depth)
        near = near + jnp.concatenate([edge_x, value[:-1]], axis=0)
        near = near + jnp.concatenate([value[1:], edge_x], axis=0)
        value = gain * near + offset
    press[...] = value[WIDE:WIDE + cx, WIDE:WIDE + cy, :]


def shapes(cx, cy, depth, thick):
    wide = [VM(thick + (cx if dx == 0 else WIDE, cy if dy == 0 else WIDE, depth), f32)
            for dx, dy in AROUND]
    return wide + wide


def slim_shapes(cx, cy, depth):
    slim = [VM((8, depth), f32) if dx and dy else VM((3, cy if dx else cx, depth), f32)
            for dx, dy in AROUND]
    return slim + slim


def body(n_x, n_y, particles, send_list, move_count, tile_pairs, tile_count, drag_tiles,
         cell_slot, fluid_velocity, pressure_init, source, solid_old, screening):
    own = particles[0, 0]
    n_own, comps, width = own.shape
    slots = send_list.shape[3]
    pool = n_own + 4 * slots
    cx, cy, depth = pressure_init.shape
    n = len(AROUND)
    send = send_list.reshape(-1)
    sds = jax.ShapeDtypeStruct
    vmem = pl.BlockSpec(memory_space=VM)
    smem = pl.BlockSpec(memory_space=pltpu.SMEM)

    blocks = pl.pallas_call(
        pick_kernel, out_shape=sds((4 * slots, comps, width), f32),
        in_specs=[smem, vmem], out_specs=vmem,
    )(send, own).reshape(4, slots, comps, width)

    ext = (cx + 2 * WIDE, cy + 2 * WIDE, depth)
    column_rows = (cx + 2) * (cy + 2) * 8
    got, columns, p_ext, g_ext, s_ext = pl.pallas_call(
        functools.partial(exchange_kernel, n_x, n_y),
        out_shape=[sds((4, slots, comps, width), f32), sds((column_rows, depth), f32),
                   sds(ext, f32), sds(ext, f32), sds(ext, f32)],
        in_specs=[vmem] * 6, out_specs=[vmem] * 5,
        scratch_shapes=shapes(cx, cy, depth, (3,)) + slim_shapes(cx, cy, depth)
        + [pltpu.SemaphoreType.DMA((2 * n + 4,)), pltpu.SemaphoreType.DMA((2 * n + 4,))],
        compiler_params=pltpu.CompilerParams(collective_id=0, has_side_effects=True,
                                             vmem_limit_bytes=LIMIT),
    )(blocks, fluid_velocity, pressure_init, screening, source, solid_old)

    deposit, force = pl.pallas_call(
        forces_kernel,
        out_shape=[sds((4, cx + 2, cy + 2, depth), f32), sds((pool, 3, width), f32)],
        in_specs=[smem] * 5 + [vmem] * 4, out_specs=[vmem] * 2,
        scratch_shapes=[pltpu.SMEM((n_own,), f32), VM((pool, comps, width), f32),
                        VM((pool, width, comps), f32), VM((pool, 16, 2 * width), bf16),
                        VM((pool, 8, width), f32), VM((pool, 8, width), f32),
                        VM((column_rows, depth), f32)],
        compiler_params=pltpu.CompilerParams(vmem_limit_bytes=LIMIT),
    )(tile_pairs.reshape(-1), tile_count.reshape(-1), drag_tiles.reshape(-1), send,
      move_count.reshape(-1), own, got, cell_slot[0, 0], columns)

    press, drag_sum = pl.pallas_call(
        functools.partial(pressure_kernel, n_x, n_y),
        out_shape=[sds((cx, cy, depth), f32), sds((3, cx, cy, depth), f32)],
        in_specs=[vmem] * 4, out_specs=[vmem] * 2,
        scratch_shapes=[VM(ext, f32)] + shapes(cx + 2, cy + 2, depth, ())
        + slim_shapes(cx, cy, depth)
        + [pltpu.SemaphoreType.DMA((2 * n,)), pltpu.SemaphoreType.DMA((2 * n,))],
        compiler_params=pltpu.CompilerParams(collective_id=1, has_side_effects=True,
                                             vmem_limit_bytes=LIMIT),
    )(deposit, p_ext, g_ext, s_ext)
    return press, drag_sum, force[None, None]


def solution(mesh):
    tail = P("gx", "gy", None)
    in_specs = (
        P("gx", "gy", None, None, None),
        P("gx", "gy", None, None),
        P("gx", "gy", None, None),
        P("gx", "gy", None, None),
        P("gx", "gy"),
        P("gx", "gy", None, None),
        P("gx", "gy", None, None),
        P(None, "gx", "gy", None),
        tail, tail, tail, tail,
    )
    out_specs = (tail, P(None, "gx", "gy", None), P("gx", "gy", None, None, None))
    return jax.shard_map(functools.partial(body, mesh.shape["gx"], mesh.shape["gy"]), mesh=mesh,
                         in_specs=in_specs, out_specs=out_specs, check_vma=False)
```
